512 devices in a mesh: blk: 16 (over x_hi, y), grp: 32 (over x_lo, z, core).
Axes of the slice: x: 4 (x_hi: 2, x_lo: 2; x = x_hi * 2 + x_lo), y: 8, z: 8, core: 2. Of those that a mesh axis runs over, the one named last changes fastest.
Arguments:
- blocks: bfloat16 [16, 32, 16, 6, 128, 128], P('blk', 'grp'), may hold values from -0.109375 to 0.109375
- block_row: int32 [16, 32, 16, 6], P('blk', 'grp'), may hold values from 0 to 3
- block_col: int32 [16, 32, 16, 6], P('blk', 'grp'), may hold values from 0 to 3
- probes: bfloat16 [262144, 256], P(('blk', 'grp')), may hold values from -6 to 6
- adjoint_probes: bfloat16 [262144, 256], P(('blk', 'grp')), may hold values from -6 to 6
- row_owner: int32 [262144, 1], P(('blk', 'grp')), may hold values from 0 to 31; in each aligned block of 512 rows (0 to 511, 512 to 1023, ...) at most 32 rows name the same one
Outputs:
- row_samples: bfloat16 [262144, 256], P(('blk', 'grp'))
- column_samples: bfloat16 [262144, 256], P(('blk', 'grp'))
- row_gram: float32 [16, 32, 256, 256], P('blk', 'grp')
- column_gram: float32 [16, 32, 256, 256], P('blk', 'grp')
The draws below stay inside these ranges and needn't reach their ends.
Inputs may be any that keep to these rules, and one draw needn't show every extreme that they name: `row_owner`: in each aligned block of 512 rows (the rows of one device) no owner is named by more than 32 rows; one owner is named by exactly 32 rows in some blocks.
All inputs are finite; a program needn't handle non-finite values.
Results may differ from the reference program's by a relative error of at most 0.018.
Values may be sent and summed in bfloat16 or wider, within the bound.
No kernel may reach another device: no remote copies, remote signals or barrier semaphores. Data moves between devices by JAX's collectives and lax.ppermute only.
A program may use at most 128 MiB of HBM per device.

```python
import math
import jax
import jax.numpy as jnp
import numpy as np
from jax import lax

BS = 128
P_SIZE = 256
BR_DEV = 4
KB_SRC = 6
ROWS_DEV = 512
NROWS = 262144
CAP = 32
N_BLK = 16
N_GRP = 32


def set_ends(values, rng, smallest, top_value):
    dims = values.shape
    spot = [jax.random.randint(jax.random.fold_in(rng, axis), (), 0, dims[axis]) for axis in range(len(dims))]
    values = values.at[tuple(spot)].set(smallest)
    longest = dims.index(max(dims))
    spot[longest] = (spot[longest] + 1) % dims[longest]
    return values.at[tuple(spot)].set(top_value)


def level_of(own_key, extent, cuts, low, high):
    gain = 1.0
    for dim, shards_of in cuts:
        draws = jax.random.uniform(jax.random.fold_in(jax.random.fold_in(own_key, 6), dim), (shards_of,), jnp.float32, low / len(cuts), high / len(cuts))
        gain = gain * jnp.repeat(jnp.exp(draws), extent[dim] // shards_of).reshape((-1,) + (1,) * (len(extent) - 1 - dim))
    return gain


def assign_block(own_key, own, number, rows, count, top, most, slope):
    ranking = jax.random.permutation(own_key, count)
    heavy_load, usual = load_shares(count, rows * top, most, slope, True), load_shares(count, rows * top, most, slope, False)
    places = jnp.arange(count)

    def named(lengths, offset_by):
        used = int((lengths > 0).sum())
        fixed = max(1, used // 4)
        passed = fixed + (places - fixed + offset_by * (used - fixed)) % max(1, count - fixed)
        return jnp.zeros((count,), jnp.int32).at[ranking[jnp.where(places < fixed, places, passed)]].set(jnp.asarray(lengths, jnp.int32))

    lengths = jnp.where(number % 4 == 0, named(heavy_load, number // 4), named(usual, number - number // 4 - 1))
    mixed = jax.random.permutation(jax.random.fold_in(own, 3), count)
    donor, taker = mixed[0:count // 2 * 2:2], mixed[1:count // 2 * 2:2]
    slack = jnp.minimum(lengths[donor] - 1, most - lengths[taker]) // 2
    slack = jnp.where((donor == ranking[0]) | (taker == ranking[0]) | (lengths[taker] == 0), 0, jnp.maximum(slack, 0))
    passed = jax.random.randint(jax.random.fold_in(own, 4), (count // 2,), 0, 1 << 20) % (slack + 1)
    lengths = lengths.at[donor].add(-passed).at[taker].add(passed)
    labels = jnp.searchsorted(jnp.cumsum(lengths), jnp.arange(rows * top), side="right").astype(jnp.int32)
    table = labels.reshape(top, rows).T
    table = table[jax.random.permutation(jax.random.fold_in(own, 1), rows)]
    offset_by = jax.random.randint(jax.random.fold_in(own, 2), (rows, 1), 0, top)
    return jnp.take_along_axis(table, (jnp.arange(top)[None, :] + offset_by) % top, axis=1)


def load_shares(count, total, most, slope, full):
    loads = [(1 << 20) // math.isqrt(rank ** slope) + 1 for rank in range(1, count + 1)]
    largest = most if full else min(most, max(-(-total // count), total * loads[0] // sum(loads)))
    least = 1 if total - largest >= count - 1 else 0
    given, rest = [largest] + [least] * (count - 1), total - largest - least * (count - 1)
    while rest > 0:
        candidates = [i for i in range(1, count) if given[i] < largest] or [i for i in range(1, count) if given[i] < most]
        mass, budget = sum([loads[i] for i in candidates]), rest
        for i in candidates:
            extra = min(most - given[i], max(1, budget * loads[i] // mass), rest)
            given[i] = given[i] + extra
            rest = rest - extra
    return np.array(given)


def normal_values(own_key, extent, scale, bound, shards=(), held_as=jnp.bfloat16):
    entries = scale * jax.random.normal(own_key, extent, jnp.float32)
    if shards:
        entries = entries * level_of(own_key, extent, shards, -0.22, 0.18)
    return jnp.clip(entries, -bound, bound).astype(held_as)


def setup_inputs(seed: int = 0) -> dict:
    key_of = jax.random.split(jax.random.key(seed), 7)
    blocks = normal_values(key_of[0], (N_BLK, N_GRP, N_BLK, KB_SRC, BS, BS), (BS * N_BLK * KB_SRC // BR_DEV) ** -0.5, 0.109375, ((0, 16), (1, 32)))
    block_row = set_ends(jax.random.randint(key_of[1], (N_BLK, N_GRP, N_BLK, KB_SRC), 0, BR_DEV), jax.random.fold_in(key_of[1], 1), 0, BR_DEV - 1).astype(jnp.int32)
    block_col = set_ends(jax.random.randint(key_of[2], (N_BLK, N_GRP, N_BLK, KB_SRC), 0, BR_DEV), jax.random.fold_in(key_of[2], 1), 0, BR_DEV - 1).astype(jnp.int32)
    probes = normal_values(key_of[3], (NROWS, P_SIZE), 1.0, 6.0, ((0, 512),))
    adjoint_probes = normal_values(key_of[4], (NROWS, P_SIZE), 1.0, 6.0, ((0, 512),))
    row_owner_keys = jax.random.split(jax.random.fold_in(key_of[5], 1), NROWS // ROWS_DEV)
    row_owner_turns = jax.random.permutation(jax.random.fold_in(key_of[5], 3), NROWS // ROWS_DEV)
    row_owner = jax.vmap(lambda own, number: assign_block(jax.random.fold_in(key_of[5], 2), own, number, ROWS_DEV, N_GRP, 1, CAP, 2))(row_owner_keys, row_owner_turns).reshape((NROWS, 1))
    return {"blocks": blocks, "block_row": block_row, "block_col": block_col, "probes": probes, "adjoint_probes": adjoint_probes, "row_owner": row_owner}


HIGHEST = lax.Precision.HIGHEST


def pack_rows(samples, owner, owners, capacity):
    member = (owner == jnp.arange(owners, dtype=jnp.int32)[None, :]).astype(jnp.int32)
    before = jnp.cumsum(member, axis=0) - member
    rank = jnp.sum(before * member, axis=1)
    slot = owner[:, 0] * capacity + rank
    return jnp.zeros((owners * capacity, samples.shape[1]), samples.dtype).at[slot].set(samples)


def single_gram(rows):
    return jnp.dot(rows.T, rows, preferred_element_type=jnp.float32)


def owner_grams(samples, row_owner):
    packed = jax.vmap(lambda s, o: pack_rows(s, o, N_GRP, CAP))(
        samples.reshape(N_BLK * N_GRP, ROWS_DEV, P_SIZE), row_owner.reshape(N_BLK * N_GRP, ROWS_DEV, 1))
    packed = packed.reshape(N_BLK, N_GRP, N_GRP, CAP, P_SIZE)
    packed = jnp.transpose(packed, (0, 2, 1, 3, 4)).reshape(N_BLK, N_GRP, N_GRP * CAP, P_SIZE)
    grams = lax.map(lambda g: jax.vmap(single_gram)(g), packed)
    return grams / ROWS_DEV


def merge_blocks(blocks_b, rows_b, cols_b):
    count = N_BLK * KB_SRC
    source = jnp.arange(N_BLK, dtype=jnp.int32)[None, :, None]
    key = (source * BR_DEV + rows_b) * BR_DEV + cols_b
    key = key.reshape(N_GRP, count)
    equal = (key[:, :, None] == key[:, None, :]).astype(jnp.float32)
    order = jnp.arange(count, dtype=jnp.int32)
    earlier = (order[None, :] < order[:, None]).astype(jnp.float32)
    first = (jnp.sum(equal * earlier[None], axis=2) == 0).astype(jnp.float32)
    flat = blocks_b.astype(jnp.float32).reshape(N_GRP, count, BS * BS)
    merged = jnp.einsum("gkl,glx->gkx", equal, flat, precision=HIGHEST) * first[:, :, None]
    merged = merged.astype(jnp.bfloat16).reshape(N_GRP, N_BLK, KB_SRC, BS, BS)
    return merged.astype(jnp.float32)


def reference(blocks, block_row, block_col, probes, adjoint_probes, row_owner):
    probe_grid = probes.reshape(N_BLK, N_GRP, BR_DEV, BS, P_SIZE)
    adjoint_grid = adjoint_probes.reshape(N_BLK, N_GRP, BR_DEV, BS, P_SIZE)
    source = jnp.arange(N_BLK, dtype=jnp.int32)[None, :, None]
    place = jnp.arange(N_GRP, dtype=jnp.int32)[:, None, None]
    choose = jnp.arange(BR_DEV, dtype=jnp.int32)

    def step(carry, inputs):
        blocks_b, rows_b, cols_b, adjoint_b = inputs
        wide = merge_blocks(blocks_b, rows_b, cols_b)
        picked = probe_grid[source, place, cols_b].astype(jnp.float32)
        product = jnp.einsum("gskij,gskjp->gskip", wide, picked, precision=HIGHEST)
        row_sel = (rows_b[..., None] == choose).astype(jnp.float32)
        forward = jnp.einsum("gskc,gskip->gcip", row_sel, product, precision=HIGHEST)
        chosen = adjoint_b[place, rows_b].astype(jnp.float32)
        back = jnp.einsum("gskji,gskjp->gskip", wide, chosen, precision=HIGHEST)
        col_sel = (cols_b[..., None] == choose).astype(jnp.float32)
        term = jnp.einsum("gskc,gskip->sgcip", col_sel, back, precision=HIGHEST)
        rounded = lax.optimization_barrier(term.astype(jnp.bfloat16))
        return carry + rounded.astype(jnp.float32), forward.astype(jnp.bfloat16)

    start = jnp.zeros((N_BLK, N_GRP, BR_DEV, BS, P_SIZE), jnp.float32)
    total, forward_all = lax.scan(step, start, (blocks, block_row, block_col, adjoint_grid))
    row_samples = forward_all.reshape(NROWS, P_SIZE)
    column_samples = total.astype(jnp.bfloat16).reshape(NROWS, P_SIZE)
    row_gram = owner_grams(row_samples, row_owner)
    column_gram = owner_grams(column_samples, row_owner)
    return (row_samples, column_samples, row_gram, column_gram)
```

```python
import functools

import jax
import jax.numpy as jnp
from jax import lax
from jax.experimental import pallas as pl
from jax.experimental.pallas import tpu as pltpu
from jax.sharding import PartitionSpec as P

F32 = jnp.float32
BF16 = jnp.bfloat16
PARTS = (3, 3, 2)


def params(mib):
    return pltpu.CompilerParams(vmem_limit_bytes=mib * 1024 * 1024)


ANY = pl.BlockSpec(memory_space=pl.ANY)
VMEM = pl.BlockSpec(memory_space=pltpu.VMEM)
SMEM = pl.BlockSpec(memory_space=pltpu.SMEM)
HBM = pl.BlockSpec(memory_space=pltpu.HBM)


def arrange_kernel(first_ref, a_ref, _, *refs):
    outs, sems = refs[:-1], refs[-1]
    copies = []
    for out, size in zip(outs, PARTS):
        for n in range(size):
            t = len(copies)
            copies.append(pltpu.make_async_copy(a_ref.at[first_ref[0] + t], out.at[n], sems.at[t]))
            copies[-1].start()
    for copy in copies:
        copy.wait()


def arrange(first, blocks, before):
    _, k, side, _ = blocks.shape
    return pl.pallas_call(
        arrange_kernel,
        in_specs=[SMEM, VMEM, ANY],
        out_specs=[HBM] * len(PARTS),
        out_shape=[pltpu.HBM((size, k, side, side), blocks.dtype) for size in PARTS],
        scratch_shapes=[pltpu.SemaphoreType.DMA((sum(PARTS),))],
        compiler_params=params(6),
        name="arrange",
    )(first, blocks, before)


def turn_kernel(q_ref, code_ref, qx_ref):
    rows, width = q_ref.shape
    qx_ref[0:width, :] = q_ref[...].T
    qx_ref[width:, :] = jnp.broadcast_to(code_ref[...], (qx_ref.shape[0] - width, rows)).astype(BF16)


def turn(q, codes):
    rows, width = q.shape
    return pl.pallas_call(
        turn_kernel,
        out_shape=jax.ShapeDtypeStruct((width + 16, rows), BF16),
        compiler_params=params(6),
        name="turn",
    )(q, codes)


def slots_kernel(owners, capacity, owner_ref, _, slot_ref):
    owner = owner_ref[...]
    rows = owner.shape[1]
    member = lax.broadcasted_iota(jnp.int32, (owners, rows), 0) == owner
    earlier = lax.broadcasted_iota(jnp.int32, (rows, rows), 0) < lax.broadcasted_iota(jnp.int32, (rows, rows), 1)
    before = jnp.dot(member.astype(BF16), earlier.astype(BF16), preferred_element_type=F32)
    rank = jnp.sum(jnp.where(member, before, 0.0), axis=0, keepdims=True)
    slot_ref[...] = owner * capacity + rank.astype(jnp.int32)


def slots_of(owner, owners, capacity, before):
    return pl.pallas_call(
        functools.partial(slots_kernel, owners, capacity),
        in_specs=[VMEM, ANY],
        out_specs=VMEM,
        out_shape=jax.ShapeDtypeStruct(owner.shape, jnp.int32),
        compiler_params=params(6),
        name="slots",
    )(owner, before)


def strip_kernel(start, first_ref, mine_ref, theirs_ref, q_ref, qp_ref, a_ref, b_ref, *refs):
    c_ref, d_ref = refs[-2:]
    k = a_ref.shape[1]
    side = a_ref.shape[2]
    rows = d_ref.shape[1] // 2
    per = rows // side
    width = c_ref.shape[1]
    d_ref[...] = jnp.zeros(d_ref.shape, d_ref.dtype)
    source = first_ref[0] + start + pl.program_id(0)
    for base, codes, blk in ((0, mine_ref, a_ref), (rows, theirs_ref, b_ref)):
        for n in range(k):
            code = codes[source * k + n]
            at_row = pl.multiple_of(base + (code // per) * side, side)
            at_col = pl.multiple_of((code % per) * side, side)
            place = (0, pl.ds(at_row, side), pl.ds(at_col, side))
            d_ref[place] = (d_ref[place].astype(F32) + blk[0, n].astype(F32)).astype(d_ref.dtype)
    term = jnp.dot(q_ref[0:width, :], d_ref[0, 0:rows, :], preferred_element_type=F32)
    term += jnp.dot(qp_ref[0:width, :], d_ref[0, rows:, :], preferred_element_type=F32)
    c_ref[0] = term.astype(c_ref.dtype)


def strips(start, first, mine, theirs, qx, qx_partner, blocks, received, width, held):
    _, k, side, _ = blocks.shape
    rows = qx.shape[1]
    size, groups = received.shape[0], sum(PARTS)
    whole = pl.BlockSpec(qx.shape, lambda i, *_: (0, 0))
    return pl.pallas_call(
        functools.partial(strip_kernel, start),
        grid_spec=pltpu.PrefetchScalarGridSpec(
            num_scalar_prefetch=3,
            grid=(size,),
            in_specs=[
                whole,
                whole,
                pl.BlockSpec((1, k, side, side), lambda i, first, *_: (first[0] + start + i, 0, 0, 0)),
                pl.BlockSpec((1, k, side, side), lambda i, *_: (i, 0, 0, 0)),
            ]
            + [HBM] * len(held),
            out_specs=[
                pl.BlockSpec((1, width, rows), lambda i, *_: (start + i, 0, 0)),
                pl.BlockSpec((1, 2 * rows, rows), lambda i, *_: (start + i, 0, 0)),
            ],
        ),
        out_shape=[
            pltpu.HBM((groups, width, rows), BF16),
            pltpu.HBM((groups, 2 * rows, rows), BF16),
        ],
        input_output_aliases={7 + n: n for n in range(len(held))},
        compiler_params=params(10),
        name="strips",
    )(first, mine, theirs, qx, qx_partner, blocks, received, *held)


def forward_kernel(d_ref, p_ref, own_ref, send_ref, total_ref):
    step = pl.program_id(0)
    rows = own_ref.shape[0]
    term = sum(jnp.dot(d_ref[n], p_ref[n], preferred_element_type=F32) for n in range(d_ref.shape[0]))

    @pl.when(step == 0)
    def _():
        total_ref[...] = term

    @pl.when(step > 0)
    def _():
        total_ref[...] += term

    @pl.when(step == pl.num_programs(0) - 1)
    def _():
        own_ref[...] = total_ref[0:rows, :]
        send_ref[...] = total_ref[rows:, :].astype(send_ref.dtype)


def forward(dense, panels):
    groups, rows, width = panels.shape
    whole = pl.BlockSpec((rows, width), lambda i: (0, 0))
    return pl.pallas_call(
        forward_kernel,
        grid=(groups // 2,),
        in_specs=[
            pl.BlockSpec((2, 2 * rows, rows), lambda i: (i, 0, 0)),
            pl.BlockSpec((2, rows, width), lambda i: (i, 0, 0)),
        ],
        out_specs=[whole, whole],
        scratch_shapes=[pltpu.VMEM((2 * rows, width), F32)],
        out_shape=[jax.ShapeDtypeStruct((rows, width), F32), jax.ShapeDtypeStruct((rows, width), BF16)],
        compiler_params=params(20),
        name="forward",
    )(pltpu.with_memory_space_constraint(dense, pltpu.HBM), panels)


def one_hot(slot, slots):
    return (lax.broadcasted_iota(jnp.int32, (slots, slot.shape[1]), 0) == slot).astype(BF16)


def pack_rows_kernel(own_ref, got_ref, slot_ref, samples_ref, packed_ref):
    samples = (own_ref[...] + got_ref[...].astype(F32)).astype(BF16)
    samples_ref[...] = samples
    packed_ref[...] = jnp.dot(
        one_hot(slot_ref[...], packed_ref.shape[0]), samples, preferred_element_type=F32
    ).astype(BF16)


def pack_rows(own, got, slot, slots):
    rows, width = own.shape
    return pl.pallas_call(
        pack_rows_kernel,
        out_shape=[jax.ShapeDtypeStruct((rows, width), BF16), jax.ShapeDtypeStruct((slots, width), BF16)],
        compiler_params=params(8),
        name="pack_rows",
    )(own, got, slot)


def pack_columns_kernel(samples_ref, slot_ref, _, packed_ref):
    packed_ref[...] = lax.dot_general(
        one_hot(slot_ref[...], packed_ref.shape[0]),
        samples_ref[...],
        (((1,), (1,)), ((), ())),
        preferred_element_type=F32,
    ).astype(BF16)


def pack_columns(samples, slot, slots, before):
    return pl.pallas_call(
        pack_columns_kernel,
        in_specs=[VMEM, VMEM, ANY],
        out_specs=VMEM,
        out_shape=jax.ShapeDtypeStruct((slots, samples.shape[0]), BF16),
        compiler_params=params(8),
        name="pack_columns",
    )(samples, slot, before)


def owner_gram(received, count):
    gram = lax.dot_general(received, received, (((0,), (0,)), ((), ())), preferred_element_type=F32)
    return (gram / count)[None, None]


def body(blocks, block_row, block_col, probes, adjoint_probes, row_owner):
    groups, per_group, side = blocks.shape[2], blocks.shape[3], blocks.shape[4]
    blocks = blocks.reshape(groups, per_group, side, side)
    n_rows, width = probes.shape
    owners = lax.axis_size("grp")
    capacity = 2 * n_rows // owners
    slots = owners * capacity
    ring = groups // 2
    half = lax.axis_index("blk") // ring
    kept, crossing = (half * ring).reshape(1), ((1 - half) * ring).reshape(1)
    across = [(b, (b + ring) % groups) for b in range(groups)]
    halves = [list(range(ring)), list(range(ring, groups))]

    codes = (block_row * (n_rows // side) + block_col).reshape(groups * per_group)
    code_row = jnp.pad(codes.astype(F32), (0, n_rows - codes.shape[0])).reshape(1, n_rows)
    qx = turn(adjoint_probes, code_row)
    leaving = arrange(crossing, blocks, qx)
    panels = lax.all_gather(probes, "blk", axis=0, tiled=True, axis_index_groups=halves).reshape(ring, n_rows, width)
    qx_partner = lax.ppermute(qx, "blk", across)
    received = [lax.ppermute(part, "blk", across) for part in leaving]
    partner_codes = qx_partner[width, 0 : codes.shape[0]].astype(jnp.int32)
    slot = slots_of(row_owner.reshape(1, n_rows), owners, capacity, partner_codes)

    held = ()
    for j in range(len(PARTS)):
        held = strips(
            sum(PARTS[:j]), kept, codes, partner_codes, qx, qx_partner, blocks, received[j], width, held
        )
    terms, dense = held
    columns = lax.psum_scatter(terms, "blk", scatter_dimension=0, tiled=False, axis_index_groups=halves)
    own, partial = forward(dense, panels)
    got = lax.ppermute(partial, "blk", across)
    row_samples, row_packed = pack_rows(own, got, slot, slots)
    row_received = lax.all_to_all(row_packed.reshape(owners, capacity, width), "grp", 0, 0, tiled=True)
    column_packed = pack_columns(columns, slot, slots, row_received)
    column_received = lax.all_to_all(column_packed.reshape(owners, capacity, width), "grp", 0, 0, tiled=True)
    row_gram = owner_gram(row_received.reshape(slots, width), n_rows)
    column_gram = owner_gram(column_received.reshape(slots, width), n_rows)
    return (row_samples, columns.T, row_gram, column_gram)


def solution(mesh):
    in_specs = (
        P("blk", "grp", None, None, None, None),
        P("blk", "grp", None, None),
        P("blk", "grp", None, None),
        P(("blk", "grp"), None),
        P(("blk", "grp"), None),
        P(("blk", "grp"), None),
    )
    out_specs = (
        P(("blk", "grp"), None),
        P(("blk", "grp"), None),
        P("blk", "grp", None, None),
        P("blk", "grp", None, None),
    )
    return jax.shard_map(body, mesh=mesh, in_specs=in_specs, out_specs=out_specs, check_vma=False)
```

```python
import functools

import jax
import jax.numpy as jnp
from jax import lax
from jax.experimental import pallas as pl
from jax.experimental.pallas import tpu as pltpu
from jax.sharding import PartitionSpec as P

F32 = jnp.float32
BF16 = jnp.bfloat16
PARTS = (3, 3, 2)


def params(mib):
    return pltpu.CompilerParams(vmem_limit_bytes=mib * 1024 * 1024)


ANY = pl.BlockSpec(memory_space=pl.ANY)
VMEM = pl.BlockSpec(memory_space=pltpu.VMEM)
SMEM = pl.BlockSpec(memory_space=pltpu.SMEM)
HBM = pl.BlockSpec(memory_space=pltpu.HBM)


def turn_kernel(q_ref, code_ref, out_ref):
    side = out_ref.shape[1]
    down, across = q_ref.shape[1] // side, q_ref.shape[0] // side
    for i in range(down):
        for j in range(across):
            out_ref[i * across + j] = q_ref[j * side : (j + 1) * side, i * side : (i + 1) * side].T
    out_ref[down * across] = jnp.broadcast_to(code_ref[...], (side, side)).astype(BF16)


def turn(q, codes):
    side = codes.shape[1]
    return pl.pallas_call(
        turn_kernel,
        out_shape=jax.ShapeDtypeStruct((q.size // side**2 + 1, side, side), BF16),
        compiler_params=params(6),
        name="turn",
    )(q, codes)


def arrange_kernel(first_ref, a_ref, q_ref, *refs):
    outs, sems = refs[:-1], refs[-1]
    k, head = a_ref.shape[1], q_ref.shape[0]
    copies = [pltpu.make_async_copy(q_ref, outs[0].at[pl.ds(0, head)], sems.at[0])]
    for j, size in enumerate(PARTS):
        for n in range(size):
            t = len(copies)
            target = outs[j].at[pl.ds((0 if j else head) + n * k, k)]
            copies.append(pltpu.make_async_copy(a_ref.at[first_ref[0] + t - 1], target, sems.at[t]))
    for copy in copies:
        copy.start()
    for copy in copies:
        copy.wait()


def arrange(first, blocks, q):
    _, k, side, _ = blocks.shape
    counts = [size * k + (0 if j else q.shape[0]) for j, size in enumerate(PARTS)]
    return pl.pallas_call(
        arrange_kernel,
        in_specs=[SMEM, VMEM, VMEM],
        out_specs=[HBM] * len(PARTS),
        out_shape=[pltpu.HBM((count, side, side), blocks.dtype) for count in counts],
        scratch_shapes=[pltpu.SemaphoreType.DMA((sum(PARTS) + 1,))],
        compiler_params=params(6),
        name="arrange",
    )(first, blocks, q)


def slots_kernel(owners, capacity, owner_ref, _, slot_ref):
    owner = owner_ref[...]
    rows = owner.shape[1]
    member = lax.broadcasted_iota(jnp.int32, (owners, rows), 0) == owner
    earlier = lax.broadcasted_iota(jnp.int32, (rows, rows), 0) < lax.broadcasted_iota(jnp.int32, (rows, rows), 1)
    before = jnp.dot(member.astype(BF16), earlier.astype(BF16), preferred_element_type=F32)
    rank = jnp.sum(jnp.where(member, before, 0.0), axis=0, keepdims=True)
    slot_ref[...] = owner * capacity + rank.astype(jnp.int32)


def slots_of(owner, owners, capacity, before):
    return pl.pallas_call(
        functools.partial(slots_kernel, owners, capacity),
        in_specs=[VMEM, ANY],
        out_specs=VMEM,
        out_shape=jax.ShapeDtypeStruct(owner.shape, jnp.int32),
        compiler_params=params(6),
        name="slots",
    )(owner, before)


def strip_kernel(start, first_ref, mine_ref, theirs_ref, q_ref, qp_ref, a_ref, b_ref, *refs):
    c_ref, d_ref = refs[-2:]
    k = a_ref.shape[1]
    side = a_ref.shape[2]
    rows = d_ref.shape[1] // 2
    per = rows // side
    head = 0 if start else q_ref.shape[0]
    d_ref[...] = jnp.zeros(d_ref.shape, d_ref.dtype)
    source = first_ref[0] + start + pl.program_id(0)
    for base, codes in ((0, mine_ref), (rows, theirs_ref)):
        for n in range(k):
            code = codes[source * k + n]
            at_row = pl.multiple_of(base + (code // per) * side, side)
            at_col = pl.multiple_of((code % per) * side, side)
            place = (0, pl.ds(at_row, side), pl.ds(at_col, side))
            block = a_ref[0, n] if base == 0 else b_ref[head + pl.program_id(0) * k + n]
            d_ref[place] = (d_ref[place].astype(F32) + block.astype(F32)).astype(d_ref.dtype)

    def turned(ref):
        down = c_ref.shape[1] // side
        return jnp.concatenate(
            [jnp.concatenate([ref[i * per + j] for j in range(per)], axis=1) for i in range(down)], axis=0
        )

    term = jnp.dot(turned(q_ref), d_ref[0, 0:rows, :], preferred_element_type=F32)
    term += jnp.dot(turned(qp_ref), d_ref[0, rows:, :], preferred_element_type=F32)
    c_ref[0] = term.astype(c_ref.dtype)


def strips(start, size, first, mine, theirs, q, opening, blocks, received, shape, held):
    _, k, side, _ = blocks.shape
    rows, width = shape
    groups = sum(PARTS)
    whole = pl.BlockSpec(q.shape, lambda i, *_: (0, 0, 0))
    return pl.pallas_call(
        functools.partial(strip_kernel, start),
        grid_spec=pltpu.PrefetchScalarGridSpec(
            num_scalar_prefetch=3,
            grid=(size,),
            in_specs=[
                whole,
                whole,
                pl.BlockSpec((1, k, side, side), lambda i, first, *_: (first[0] + start + i, 0, 0, 0)),
                pl.BlockSpec(received.shape, lambda i, *_: (0, 0, 0)),
            ]
            + [HBM] * len(held),
            out_specs=[
                pl.BlockSpec((1, width, rows), lambda i, *_: (start + i, 0, 0)),
                pl.BlockSpec((1, 2 * rows, rows), lambda i, *_: (start + i, 0, 0)),
            ],
        ),
        out_shape=[
            pltpu.HBM((groups, width, rows), BF16),
            pltpu.HBM((groups, 2 * rows, rows), BF16),
        ],
        input_output_aliases={7 + n: n for n in range(len(held))},
        compiler_params=params(10),
        name="strips",
    )(first, mine, theirs, q, opening, blocks, received, *held)


def forward_kernel(d_ref, p_ref, own_ref, send_ref, total_ref):
    step = pl.program_id(0)
    rows = own_ref.shape[0]
    term = sum(jnp.dot(d_ref[n], p_ref[n], preferred_element_type=F32) for n in range(d_ref.shape[0]))

    @pl.when(step == 0)
    def _():
        total_ref[...] = term

    @pl.when(step > 0)
    def _():
        total_ref[...] += term

    @pl.when(step == pl.num_programs(0) - 1)
    def _():
        own_ref[...] = total_ref[0:rows, :]
        send_ref[...] = total_ref[rows:, :].astype(send_ref.dtype)


def forward(dense, panels):
    groups, rows, width = panels.shape
    whole = pl.BlockSpec((rows, width), lambda i: (0, 0))
    return pl.pallas_call(
        forward_kernel,
        grid=(groups // 2,),
        in_specs=[
            pl.BlockSpec((2, 2 * rows, rows), lambda i: (i, 0, 0)),
            pl.BlockSpec((2, rows, width), lambda i: (i, 0, 0)),
        ],
        out_specs=[whole, whole],
        scratch_shapes=[pltpu.VMEM((2 * rows, width), F32)],
        out_shape=[jax.ShapeDtypeStruct((rows, width), F32), jax.ShapeDtypeStruct((rows, width), BF16)],
        compiler_params=params(20),
        name="forward",
    )(pltpu.with_memory_space_constraint(dense, pltpu.HBM), panels)


def one_hot(slot, slots):
    return (lax.broadcasted_iota(jnp.int32, (slots, slot.shape[1]), 0) == slot).astype(BF16)


def pack_rows_kernel(own_ref, got_ref, slot_ref, samples_ref, packed_ref):
    samples = (own_ref[...] + got_ref[...].astype(F32)).astype(BF16)
    samples_ref[...] = samples
    packed_ref[...] = jnp.dot(
        one_hot(slot_ref[...], packed_ref.shape[0]), samples, preferred_element_type=F32
    ).astype(BF16)


def pack_rows(own, got, slot, slots):
    rows, width = own.shape
    return pl.pallas_call(
        pack_rows_kernel,
        out_shape=[jax.ShapeDtypeStruct((rows, width), BF16), jax.ShapeDtypeStruct((slots, width), BF16)],
        compiler_params=params(8),
        name="pack_rows",
    )(own, got, slot)


def pack_columns_kernel(samples_ref, slot_ref, _, packed_ref):
    packed_ref[...] = lax.dot_general(
        one_hot(slot_ref[...], packed_ref.shape[0]),
        samples_ref[...],
        (((1,), (1,)), ((), ())),
        preferred_element_type=F32,
    ).astype(BF16)


def pack_columns(samples, slot, slots, before):
    return pl.pallas_call(
        pack_columns_kernel,
        in_specs=[VMEM, VMEM, ANY],
        out_specs=VMEM,
        out_shape=jax.ShapeDtypeStruct((slots, samples.shape[0]), BF16),
        compiler_params=params(8),
        name="pack_columns",
    )(samples, slot, before)


def owner_gram(received, count):
    gram = lax.dot_general(received, received, (((0,), (0,)), ((), ())), preferred_element_type=F32)
    return (gram / count)[None, None]


def body(blocks, block_row, block_col, probes, adjoint_probes, row_owner):
    groups, per_group, side = blocks.shape[2], blocks.shape[3], blocks.shape[4]
    blocks = blocks.reshape(groups, per_group, side, side)
    n_rows, width = probes.shape
    owners = lax.axis_size("grp")
    capacity = 2 * n_rows // owners
    slots = owners * capacity
    ring = groups // 2
    half = lax.axis_index("blk") // ring
    kept, crossing = (half * ring).reshape(1), ((1 - half) * ring).reshape(1)
    across = [(b, (b + ring) % groups) for b in range(groups)]
    halves = [list(range(ring)), list(range(ring, groups))]

    codes = (block_row * (n_rows // side) + block_col).reshape(groups * per_group)
    code_row = jnp.pad(codes.astype(F32), (0, side - codes.shape[0])).reshape(1, side)
    q = turn(adjoint_probes, code_row)
    leaving = arrange(crossing, blocks, q)
    panels = lax.all_gather(probes, "blk", axis=0, tiled=True, axis_index_groups=halves).reshape(ring, n_rows, width)
    received = [lax.ppermute(part, "blk", across) for part in leaving]
    partner_codes = received[0][q.shape[0] - 1, 0, 0 : codes.shape[0]].astype(jnp.int32)
    slot = slots_of(row_owner.reshape(1, n_rows), owners, capacity, partner_codes)

    held = ()
    for j, size in enumerate(PARTS):
        held = strips(
            sum(PARTS[:j]), size, kept, codes, partner_codes, q, received[0], blocks, received[j], (n_rows, width), held
        )
    terms, dense = held
    columns = lax.psum_scatter(terms, "blk", scatter_dimension=0, tiled=False, axis_index_groups=halves)
    own, partial = forward(dense, panels)
    got = lax.ppermute(partial, "blk", across)
    row_samples, row_packed = pack_rows(own, got, slot, slots)
    row_received = lax.all_to_all(row_packed.reshape(owners, capacity, width), "grp", 0, 0, tiled=True)
    column_packed = pack_columns(columns, slot, slots, row_received)
    column_received = lax.all_to_all(column_packed.reshape(owners, capacity, width), "grp", 0, 0, tiled=True)
    row_gram = owner_gram(row_received.reshape(slots, width), n_rows)
    column_gram = owner_gram(column_received.reshape(slots, width), n_rows)
    return (row_samples, columns.T, row_gram, column_gram)


def solution(mesh):
    in_specs = (
        P("blk", "grp", None, None, None, None),
        P("blk", "grp", None, None),
        P("blk", "grp", None, None),
        P(("blk", "grp"), None),
        P(("blk", "grp"), None),
        P(("blk", "grp"), None),
    )
    out_specs = (
        P(("blk", "grp"), None),
        P(("blk", "grp"), None),
        P("blk", "grp", None, None),
        P("blk", "grp", None, None),
    )
    return jax.shard_map(body, mesh=mesh, in_specs=in_specs, out_specs=out_specs, check_vma=False)
```

```python
import functools

import jax
import jax.numpy as jnp
from jax import lax
from jax.experimental import pallas as pl
from jax.experimental.pallas import tpu as pltpu
from jax.sharding import PartitionSpec as P

F32 = jnp.float32
BF16 = jnp.bfloat16
PARTS = (3, 3, 1, 1)


def params(mib):
    return pltpu.CompilerParams(vmem_limit_bytes=mib * 1024 * 1024)


ANY = pl.BlockSpec(memory_space=pl.ANY)
VMEM = pl.BlockSpec(memory_space=pltpu.VMEM)
SMEM = pl.BlockSpec(memory_space=pltpu.SMEM)
HBM = pl.BlockSpec(memory_space=pltpu.HBM)


def prepare_kernel(first_ref, a_ref, q_ref, code_ref, own_ref, *refs):
    outs, (a_buf, q_buf, in_sems, out_sems) = refs[:-4], refs[-4:]
    k, side = a_buf.shape[1:3]
    head, groups = own_ref.shape[0], a_buf.shape[0]
    q_in = pltpu.make_async_copy(q_ref, q_buf, in_sems.at[groups])
    a_in = [pltpu.make_async_copy(a_ref.at[first_ref[0] + t], a_buf.at[t], in_sems.at[t]) for t in range(groups)]
    for copy in [q_in] + a_in:
        copy.start()
    q_in.wait()
    down, across = q_buf.shape[1] // side, q_buf.shape[0] // side
    for i in range(down):
        for j in range(across):
            own_ref[i * across + j] = q_buf[j * side : (j + 1) * side, i * side : (i + 1) * side].T
    own_ref[down * across] = jnp.broadcast_to(code_ref[...], (side, side)).astype(BF16)
    copies = [pltpu.make_async_copy(own_ref, outs[0].at[pl.ds(0, head)], out_sems.at[groups])]
    copies[0].start()
    t = 0
    for j, size in enumerate(PARTS):
        for n in range(size):
            a_in[t].wait()
            target = outs[j].at[pl.ds((0 if j else head) + n * k, k)]
            copies.append(pltpu.make_async_copy(a_buf.at[t], target, out_sems.at[t]))
            copies[-1].start()
            t += 1
    for copy in copies:
        copy.wait()


def prepare(first, blocks, q, codes):
    _, k, side, _ = blocks.shape
    head, groups = q.size // side**2 + 1, sum(PARTS)
    counts = [size * k + (0 if j else head) for j, size in enumerate(PARTS)]
    found = pl.pallas_call(
        prepare_kernel,
        in_specs=[SMEM, HBM, HBM, VMEM],
        out_specs=[VMEM] + [HBM] * len(PARTS),
        out_shape=[jax.ShapeDtypeStruct((head, side, side), BF16)]
        + [pltpu.HBM((count, side, side), blocks.dtype) for count in counts],
        scratch_shapes=[
            pltpu.VMEM((groups, k, side, side), blocks.dtype),
            pltpu.VMEM(q.shape, q.dtype),
            pltpu.SemaphoreType.DMA((groups + 1,)),
            pltpu.SemaphoreType.DMA((groups + 1,)),
        ],
        compiler_params=params(8),
        name="prepare",
    )(
        first,
        pltpu.with_memory_space_constraint(blocks, pltpu.HBM),
        pltpu.with_memory_space_constraint(q, pltpu.HBM),
        codes,
    )
    return found[0], found[1:]


def slots_kernel(owners, capacity, owner_ref, _, slot_ref):
    owner = owner_ref[...]
    rows = owner.shape[1]
    member = lax.broadcasted_iota(jnp.int32, (owners, rows), 0) == owner
    earlier = lax.broadcasted_iota(jnp.int32, (rows, rows), 0) < lax.broadcasted_iota(jnp.int32, (rows, rows), 1)
    before = jnp.dot(member.astype(BF16), earlier.astype(BF16), preferred_element_type=F32)
    rank = jnp.sum(jnp.where(member, before, 0.0), axis=0, keepdims=True)
    slot_ref[...] = owner * capacity + rank.astype(jnp.int32)


def slots_of(owner, owners, capacity, before):
    return pl.pallas_call(
        functools.partial(slots_kernel, owners, capacity),
        in_specs=[VMEM, ANY],
        out_specs=VMEM,
        out_shape=jax.ShapeDtypeStruct(owner.shape, jnp.int32),
        compiler_params=params(6),
        name="slots",
    )(owner, before)


def strip_kernel(start, first_ref, mine_ref, theirs_ref, q_ref, qp_ref, a_ref, b_ref, *refs):
    c_ref, d_ref = refs[-2:]
    k = a_ref.shape[1]
    side = a_ref.shape[2]
    rows = d_ref.shape[1] // 2
    per = rows // side
    head = 0 if start else q_ref.shape[0]
    d_ref[...] = jnp.zeros(d_ref.shape, d_ref.dtype)
    source = first_ref[0] + start + pl.program_id(0)
    for base, codes in ((0, mine_ref), (rows, theirs_ref)):
        for n in range(k):
            code = codes[source * k + n]
            at_row = pl.multiple_of(base + (code // per) * side, side)
            at_col = pl.multiple_of((code % per) * side, side)
            place = (0, pl.ds(at_row, side), pl.ds(at_col, side))
            block = a_ref[0, n] if base == 0 else b_ref[head + pl.program_id(0) * k + n]
            d_ref[place] = (d_ref[place].astype(F32) + block.astype(F32)).astype(d_ref.dtype)

    def turned(ref):
        down = c_ref.shape[1] // side
        return jnp.concatenate(
            [jnp.concatenate([ref[i * per + j] for j in range(per)], axis=1) for i in range(down)], axis=0
        )

    term = jnp.dot(turned(q_ref), d_ref[0, 0:rows, :], preferred_element_type=F32)
    term += jnp.dot(turned(qp_ref), d_ref[0, rows:, :], preferred_element_type=F32)
    c_ref[0] = term.astype(c_ref.dtype)


def strips(start, size, first, mine, theirs, q, opening, blocks, received, shape, held):
    _, k, side, _ = blocks.shape
    rows, width = shape
    groups = sum(PARTS)
    whole = pl.BlockSpec(q.shape, lambda i, *_: (0, 0, 0))
    return pl.pallas_call(
        functools.partial(strip_kernel, start),
        grid_spec=pltpu.PrefetchScalarGridSpec(
            num_scalar_prefetch=3,
            grid=(size,),
            in_specs=[
                whole,
                whole,
                pl.BlockSpec((1, k, side, side), lambda i, first, *_: (first[0] + start + i, 0, 0, 0)),
                pl.BlockSpec(received.shape, lambda i, *_: (0, 0, 0)),
            ]
            + [HBM] * len(held),
            out_specs=[
                pl.BlockSpec((1, width, rows), lambda i, *_: (start + i, 0, 0)),
                pl.BlockSpec((1, 2 * rows, rows), lambda i, *_: (start + i, 0, 0)),
            ],
        ),
        out_shape=[
            pltpu.HBM((groups, width, rows), BF16),
            pltpu.HBM((groups, 2 * rows, rows), BF16),
        ],
        input_output_aliases={7 + n: n for n in range(len(held))},
        compiler_params=params(10),
        name="strips",
    )(first, mine, theirs, q, opening, blocks, received, *held)


def forward_kernel(d_ref, p_ref, own_ref, send_ref, total_ref):
    step = pl.program_id(0)
    rows = own_ref.shape[0]
    term = sum(jnp.dot(d_ref[n], p_ref[n], preferred_element_type=F32) for n in range(d_ref.shape[0]))

    @pl.when(step == 0)
    def _():
        total_ref[...] = term

    @pl.when(step > 0)
    def _():
        total_ref[...] += term

    @pl.when(step == pl.num_programs(0) - 1)
    def _():
        own_ref[...] = total_ref[0:rows, :]
        send_ref[...] = total_ref[rows:, :].astype(send_ref.dtype)


def forward(dense, panels):
    groups, rows, width = panels.shape
    whole = pl.BlockSpec((rows, width), lambda i: (0, 0))
    return pl.pallas_call(
        forward_kernel,
        grid=(groups // 2,),
        in_specs=[
            pl.BlockSpec((2, 2 * rows, rows), lambda i: (i, 0, 0)),
            pl.BlockSpec((2, rows, width), lambda i: (i, 0, 0)),
        ],
        out_specs=[whole, whole],
        scratch_shapes=[pltpu.VMEM((2 * rows, width), F32)],
        out_shape=[jax.ShapeDtypeStruct((rows, width), F32), jax.ShapeDtypeStruct((rows, width), BF16)],
        compiler_params=params(20),
        name="forward",
    )(pltpu.with_memory_space_constraint(dense, pltpu.HBM), panels)


def one_hot(slot, slots):
    return (lax.broadcasted_iota(jnp.int32, (slots, slot.shape[1]), 0) == slot).astype(BF16)


def pack_rows_kernel(own_ref, got_ref, slot_ref, samples_ref, packed_ref):
    samples = (own_ref[...] + got_ref[...].astype(F32)).astype(BF16)
    samples_ref[...] = samples
    packed_ref[...] = jnp.dot(
        one_hot(slot_ref[...], packed_ref.shape[0]), samples, preferred_element_type=F32
    ).astype(BF16)


def pack_rows(own, got, slot, slots):
    rows, width = own.shape
    return pl.pallas_call(
        pack_rows_kernel,
        out_shape=[jax.ShapeDtypeStruct((rows, width), BF16), jax.ShapeDtypeStruct((slots, width), BF16)],
        compiler_params=params(8),
        name="pack_rows",
    )(own, got, slot)


def pack_columns_kernel(samples_ref, slot_ref, _, packed_ref):
    packed_ref[...] = lax.dot_general(
        one_hot(slot_ref[...], packed_ref.shape[0]),
        samples_ref[...],
        (((1,), (1,)), ((), ())),
        preferred_element_type=F32,
    ).astype(BF16)


def pack_columns(samples, slot, slots, before):
    return pl.pallas_call(
        pack_columns_kernel,
        in_specs=[VMEM, VMEM, ANY],
        out_specs=VMEM,
        out_shape=jax.ShapeDtypeStruct((slots, samples.shape[0]), BF16),
        compiler_params=params(8),
        name="pack_columns",
    )(samples, slot, before)


def owner_gram(received, count):
    gram = lax.dot_general(received, received, (((0,), (0,)), ((), ())), preferred_element_type=F32)
    return (gram / count)[None, None]


def body(blocks, block_row, block_col, probes, adjoint_probes, row_owner):
    groups, per_group, side = blocks.shape[2], blocks.shape[3], blocks.shape[4]
    blocks = blocks.reshape(groups, per_group, side, side)
    n_rows, width = probes.shape
    owners = lax.axis_size("grp")
    capacity = 2 * n_rows // owners
    slots = owners * capacity
    ring = groups // 2
    half = lax.axis_index("blk") // ring
    kept, crossing = (half * ring).reshape(1), ((1 - half) * ring).reshape(1)
    across = [(b, (b + ring) % groups) for b in range(groups)]
    halves = [list(range(ring)), list(range(ring, groups))]

    codes = (block_row * (n_rows // side) + block_col).reshape(groups * per_group)
    code_row = jnp.pad(codes.astype(F32), (0, side - codes.shape[0])).reshape(1, side)
    q, leaving = prepare(crossing, blocks, adjoint_probes, code_row)
    panels = lax.all_gather(probes, "blk", axis=0, tiled=True, axis_index_groups=halves).reshape(ring, n_rows, width)
    received = [lax.ppermute(part, "blk", across) for part in leaving]
    partner_codes = received[0][q.shape[0] - 1, 0, 0 : codes.shape[0]].astype(jnp.int32)
    slot = slots_of(row_owner.reshape(1, n_rows), owners, capacity, partner_codes)

    held = ()
    for j, size in enumerate(PARTS):
        held = strips(
            sum(PARTS[:j]), size, kept, codes, partner_codes, q, received[0], blocks, received[j], (n_rows, width), held
        )
    terms, dense = held
    columns = lax.psum_scatter(terms, "blk", scatter_dimension=0, tiled=False, axis_index_groups=halves)
    own, partial = forward(dense, panels)
    got = lax.ppermute(partial, "blk", across)
    row_samples, row_packed = pack_rows(own, got, slot, slots)
    row_received = lax.all_to_all(row_packed.reshape(owners, capacity, width), "grp", 0, 0, tiled=True)
    column_packed = pack_columns(columns, slot, slots, row_received)
    column_received = lax.all_to_all(column_packed.reshape(owners, capacity, width), "grp", 0, 0, tiled=True)
    row_gram = owner_gram(row_received.reshape(slots, width), n_rows)
    column_gram = owner_gram(column_received.reshape(slots, width), n_rows)
    return (row_samples, columns.T, row_gram, column_gram)


def solution(mesh):
    in_specs = (
        P("blk", "grp", None, None, None, None),
        P("blk", "grp", None, None),
        P("blk", "grp", None, None),
        P(("blk", "grp"), None),
        P(("blk", "grp"), None),
        P(("blk", "grp"), None),
    )
    out_specs = (
        P(("blk", "grp"), None),
        P(("blk", "grp"), None),
        P("blk", "grp", None, None),
        P("blk", "grp", None, None),
    )
    return jax.shard_map(body, mesh=mesh, in_specs=in_specs, out_specs=out_specs, check_vma=False)
```

```python
import functools

import jax
import jax.numpy as jnp
from jax import lax
from jax.experimental import pallas as pl
from jax.experimental.pallas import tpu as pltpu
from jax.sharding import PartitionSpec as P

F32 = jnp.float32
BF16 = jnp.bfloat16
PARTS = (3, 3, 1, 1)


def params(mib):
    return pltpu.CompilerParams(vmem_limit_bytes=mib * 1024 * 1024)


ANY = pl.BlockSpec(memory_space=pl.ANY)
VMEM = pl.BlockSpec(memory_space=pltpu.VMEM)
SMEM = pl.BlockSpec(memory_space=pltpu.SMEM)
HBM = pl.BlockSpec(memory_space=pltpu.HBM)


def prepare_kernel(first_ref, a_ref, q_ref, code_ref, own_ref, *refs):
    outs, (a_buf, q_buf, in_sems, out_sems) = refs[:-4], refs[-4:]
    k, side = a_buf.shape[1:3]
    head, groups = own_ref.shape[0], a_buf.shape[0]
    q_in = pltpu.make_async_copy(q_ref, q_buf, in_sems.at[groups])
    a_in = [pltpu.make_async_copy(a_ref.at[first_ref[0] + t], a_buf.at[t], in_sems.at[t]) for t in range(groups)]
    for copy in [q_in] + a_in:
        copy.start()
    q_in.wait()
    down, across = q_buf.shape[1] // side, q_buf.shape[0] // side
    for i in range(down):
        for j in range(across):
            own_ref[i * across + j] = q_buf[j * side : (j + 1) * side, i * side : (i + 1) * side].T
    own_ref[down * across] = jnp.broadcast_to(code_ref[...], (side, side)).astype(BF16)
    copies = [pltpu.make_async_copy(own_ref, outs[0].at[pl.ds(0, head)], out_sems.at[groups])]
    copies[0].start()
    t = 0
    for j, size in enumerate(PARTS):
        for n in range(size):
            a_in[t].wait()
            target = outs[j].at[pl.ds((0 if j else head) + n * k, k)]
            copies.append(pltpu.make_async_copy(a_buf.at[t], target, out_sems.at[t]))
            copies[-1].start()
            t += 1
    for copy in copies:
        copy.wait()


def prepare(first, blocks, q, codes):
    _, k, side, _ = blocks.shape
    head, groups = q.size // side**2 + 1, sum(PARTS)
    counts = [size * k + (0 if j else head) for j, size in enumerate(PARTS)]
    found = pl.pallas_call(
        prepare_kernel,
        in_specs=[SMEM, HBM, HBM, VMEM],
        out_specs=[VMEM] + [HBM] * len(PARTS),
        out_shape=[jax.ShapeDtypeStruct((head, side, side), BF16)]
        + [pltpu.HBM((count, side, side), blocks.dtype) for count in counts],
        scratch_shapes=[
            pltpu.VMEM((groups, k, side, side), blocks.dtype),
            pltpu.VMEM(q.shape, q.dtype),
            pltpu.SemaphoreType.DMA((groups + 1,)),
            pltpu.SemaphoreType.DMA((groups + 1,)),
        ],
        compiler_params=params(8),
        name="prepare",
    )(
        first,
        pltpu.with_memory_space_constraint(blocks, pltpu.HBM),
        pltpu.with_memory_space_constraint(q, pltpu.HBM),
        codes,
    )
    return found[0], found[1:]


def slots_kernel(owners, capacity, owner_ref, _, slot_ref):
    owner = owner_ref[...]
    rows = owner.shape[1]
    member = lax.broadcasted_iota(jnp.int32, (owners, rows), 0) == owner
    earlier = lax.broadcasted_iota(jnp.int32, (rows, rows), 0) < lax.broadcasted_iota(jnp.int32, (rows, rows), 1)
    before = jnp.dot(member.astype(BF16), earlier.astype(BF16), preferred_element_type=F32)
    rank = jnp.sum(jnp.where(member, before, 0.0), axis=0, keepdims=True)
    slot_ref[...] = owner * capacity + rank.astype(jnp.int32)


def slots_of(owner, owners, capacity, before):
    return pl.pallas_call(
        functools.partial(slots_kernel, owners, capacity),
        in_specs=[VMEM, ANY],
        out_specs=VMEM,
        out_shape=jax.ShapeDtypeStruct(owner.shape, jnp.int32),
        compiler_params=params(6),
        name="slots",
    )(owner, before)


def strip_kernel(start, first_ref, mine_ref, theirs_ref, q_ref, qp_ref, a_ref, b_ref, *refs):
    c_ref, d_ref = refs[-2:]
    k = a_ref.shape[1]
    side = a_ref.shape[2]
    rows = d_ref.shape[1] // 2
    per = rows // side
    head = 0 if start else q_ref.shape[0]
    d_ref[...] = jnp.zeros(d_ref.shape, d_ref.dtype)
    source = first_ref[0] + start + pl.program_id(0)
    for base, codes in ((0, mine_ref), (rows, theirs_ref)):
        for n in range(k):
            code = codes[source * k + n]
            at_row = pl.multiple_of(base + (code // per) * side, side)
            at_col = pl.multiple_of((code % per) * side, side)
            place = (0, pl.ds(at_row, side), pl.ds(at_col, side))
            block = a_ref[0, n] if base == 0 else b_ref[head + pl.program_id(0) * k + n]
            d_ref[place] = (d_ref[place].astype(F32) + block.astype(F32)).astype(d_ref.dtype)

    def turned(ref):
        down = c_ref.shape[1] // side
        return jnp.concatenate(
            [jnp.concatenate([ref[i * per + j] for j in range(per)], axis=1) for i in range(down)], axis=0
        )

    term = jnp.dot(turned(q_ref), d_ref[0, 0:rows, :], preferred_element_type=F32)
    term += jnp.dot(turned(qp_ref), d_ref[0, rows:, :], preferred_element_type=F32)
    c_ref[0] = term.astype(c_ref.dtype)


def strips(start, size, first, mine, theirs, q, opening, blocks, received, shape, held):
    _, k, side, _ = blocks.shape
    rows, width = shape
    groups = sum(PARTS)
    whole = pl.BlockSpec(q.shape, lambda i, *_: (0, 0, 0))
    return pl.pallas_call(
        functools.partial(strip_kernel, start),
        grid_spec=pltpu.PrefetchScalarGridSpec(
            num_scalar_prefetch=3,
            grid=(size,),
            in_specs=[
                whole,
                whole,
                pl.BlockSpec((1, k, side, side), lambda i, first, *_: (first[0] + start + i, 0, 0, 0)),
                pl.BlockSpec(received.shape, lambda i, *_: (0, 0, 0)),
            ]
            + [HBM] * len(held),
            out_specs=[
                pl.BlockSpec((1, width, rows), lambda i, *_: (start + i, 0, 0)),
                pl.BlockSpec((1, 2 * rows, rows), lambda i, *_: (start + i, 0, 0)),
            ],
        ),
        out_shape=[
            pltpu.HBM((groups, width, rows), BF16),
            pltpu.HBM((groups, 2 * rows, rows), BF16),
        ],
        input_output_aliases={7 + n: n for n in range(len(held))},
        compiler_params=params(10),
        name="strips",
    )(first, mine, theirs, q, opening, blocks, received, *held)


def forward_kernel(d_ref, p_ref, _, out_ref, total_ref):
    step = pl.program_id(0)
    term = sum(jnp.dot(d_ref[n], p_ref[n], preferred_element_type=F32) for n in range(d_ref.shape[0]))

    @pl.when(step == 0)
    def _():
        total_ref[...] = term

    @pl.when(step > 0)
    def _():
        total_ref[...] += term

    @pl.when(step == pl.num_programs(0) - 1)
    def _():
        out_ref[...] = total_ref[...].astype(out_ref.dtype)


def forward(dense, panels, half, dtype, before):
    groups, rows, width = panels.shape
    return pl.pallas_call(
        forward_kernel,
        grid=(groups // 2,),
        in_specs=[
            pl.BlockSpec((2, rows, rows), lambda i: (i, half, 0)),
            pl.BlockSpec((2, rows, width), lambda i: (i, 0, 0)),
            ANY,
        ],
        out_specs=pl.BlockSpec((rows, width), lambda i: (0, 0)),
        scratch_shapes=[pltpu.VMEM((rows, width), F32)],
        out_shape=jax.ShapeDtypeStruct((rows, width), dtype),
        compiler_params=params(12),
        name="forward",
    )(pltpu.with_memory_space_constraint(dense, pltpu.HBM), pltpu.with_memory_space_constraint(panels, pltpu.HBM), before)


def one_hot(slot, slots):
    return (lax.broadcasted_iota(jnp.int32, (slots, slot.shape[1]), 0) == slot).astype(BF16)


def pack_rows_kernel(own_ref, got_ref, slot_ref, samples_ref, packed_ref):
    samples = (own_ref[...] + got_ref[...].astype(F32)).astype(BF16)
    samples_ref[...] = samples
    packed_ref[...] = jnp.dot(
        one_hot(slot_ref[...], packed_ref.shape[0]), samples, preferred_element_type=F32
    ).astype(BF16)


def pack_rows(own, got, slot, slots):
    rows, width = own.shape
    return pl.pallas_call(
        pack_rows_kernel,
        out_shape=[jax.ShapeDtypeStruct((rows, width), BF16), jax.ShapeDtypeStruct((slots, width), BF16)],
        compiler_params=params(8),
        name="pack_rows",
    )(own, got, slot)


def pack_columns_kernel(samples_ref, slot_ref, _, packed_ref, held_ref, sem):
    copy = pltpu.make_async_copy(samples_ref, held_ref, sem)
    copy.start()
    chosen = one_hot(slot_ref[...], packed_ref.shape[0])
    copy.wait()
    packed_ref[...] = lax.dot_general(
        chosen, held_ref[...], (((1,), (1,)), ((), ())), preferred_element_type=F32
    ).astype(BF16)


def pack_columns(samples, slot, slots, before):
    return pl.pallas_call(
        pack_columns_kernel,
        in_specs=[HBM, VMEM, ANY],
        out_specs=VMEM,
        out_shape=jax.ShapeDtypeStruct((slots, samples.shape[0]), BF16),
        scratch_shapes=[pltpu.VMEM(samples.shape, BF16), pltpu.SemaphoreType.DMA],
        compiler_params=params(8),
        name="pack_columns",
    )(pltpu.with_memory_space_constraint(samples, pltpu.HBM), slot, before)


def owner_gram(received, count):
    gram = lax.dot_general(received, received, (((0,), (0,)), ((), ())), preferred_element_type=F32)
    return (gram / count)[None, None]


def body(blocks, block_row, block_col, probes, adjoint_probes, row_owner):
    groups, per_group, side = blocks.shape[2], blocks.shape[3], blocks.shape[4]
    blocks = blocks.reshape(groups, per_group, side, side)
    n_rows, width = probes.shape
    owners = lax.axis_size("grp")
    capacity = 2 * n_rows // owners
    slots = owners * capacity
    ring = groups // 2
    half = lax.axis_index("blk") // ring
    kept, crossing = (half * ring).reshape(1), ((1 - half) * ring).reshape(1)
    across = [(b, (b + ring) % groups) for b in range(groups)]
    halves = [list(range(ring)), list(range(ring, groups))]

    codes = (block_row * (n_rows // side) + block_col).reshape(groups * per_group)
    code_row = jnp.pad(codes.astype(F32), (0, side - codes.shape[0])).reshape(1, side)
    q, leaving = prepare(crossing, blocks, adjoint_probes, code_row)
    panels = lax.all_gather(probes, "blk", axis=0, tiled=True, axis_index_groups=halves).reshape(ring, n_rows, width)
    received = [lax.ppermute(part, "blk", across) for part in leaving]
    partner_codes = received[0][q.shape[0] - 1, 0, 0 : codes.shape[0]].astype(jnp.int32)
    slot = slots_of(row_owner.reshape(1, n_rows), owners, capacity, partner_codes)

    held = ()
    for j, size in enumerate(PARTS):
        held = strips(
            sum(PARTS[:j]), size, kept, codes, partner_codes, q, received[0], blocks, received[j], (n_rows, width), held
        )
    terms, dense = held
    columns = lax.psum_scatter(terms, "blk", scatter_dimension=0, tiled=False, axis_index_groups=halves)
    partial = forward(dense, panels, 1, BF16, slot)
    own = forward(dense, panels, 0, F32, partial)
    got = lax.ppermute(partial, "blk", across)
    row_samples, row_packed = pack_rows(own, got, slot, slots)
    row_received = lax.all_to_all(row_packed.reshape(owners, capacity, width), "grp", 0, 0, tiled=True)
    column_packed = pack_columns(columns, slot, slots, row_received)
    column_received = lax.all_to_all(column_packed.reshape(owners, capacity, width), "grp", 0, 0, tiled=True)
    row_gram = owner_gram(row_received.reshape(slots, width), n_rows)
    column_gram = owner_gram(column_received.reshape(slots, width), n_rows)
    return (row_samples, columns.T, row_gram, column_gram)


def solution(mesh):
    in_specs = (
        P("blk", "grp", None, None, None, None),
        P("blk", "grp", None, None),
        P("blk", "grp", None, None),
        P(("blk", "grp"), None),
        P(("blk", "grp"), None),
        P(("blk", "grp"), None),
    )
    out_specs = (
        P(("blk", "grp"), None),
        P(("blk", "grp"), None),
        P("blk", "grp", None, None),
        P("blk", "grp", None, None),
    )
    return jax.shard_map(body, mesh=mesh, in_specs=in_specs, out_specs=out_specs, check_vma=False)
```

```python
import functools

import jax
import jax.numpy as jnp
from jax import lax
from jax.experimental import pallas as pl
from jax.experimental.pallas import tpu as pltpu
from jax.sharding import PartitionSpec as P

F32 = jnp.float32
BF16 = jnp.bfloat16
PARTS = (3, 3, 2)


def params(mib):
    return pltpu.CompilerParams(vmem_limit_bytes=mib * 1024 * 1024)


ANY = pl.BlockSpec(memory_space=pl.ANY)
VMEM = pl.BlockSpec(memory_space=pltpu.VMEM)
SMEM = pl.BlockSpec(memory_space=pltpu.SMEM)
HBM = pl.BlockSpec(memory_space=pltpu.HBM)


def prepare_kernel(first_ref, a_ref, q_ref, code_ref, own_ref, *refs):
    outs, (a_buf, q_buf, in_sems, out_sems) = refs[:-4], refs[-4:]
    k, side = a_buf.shape[1:3]
    head, groups = own_ref.shape[0], a_buf.shape[0]
    q_in = pltpu.make_async_copy(q_ref, q_buf, in_sems.at[groups])
    a_in = [pltpu.make_async_copy(a_ref.at[first_ref[0] + t], a_buf.at[t], in_sems.at[t]) for t in range(groups)]
    for copy in [q_in] + a_in:
        copy.start()
    q_in.wait()
    down, across = q_buf.shape[1] // side, q_buf.shape[0] // side
    for i in range(down):
        for j in range(across):
            own_ref[i * across + j] = q_buf[j * side : (j + 1) * side, i * side : (i + 1) * side].T
    own_ref[down * across] = jnp.broadcast_to(code_ref[...], (side, side)).astype(BF16)
    copies = [pltpu.make_async_copy(own_ref, outs[0].at[pl.ds(0, head)], out_sems.at[groups])]
    copies[0].start()
    t = 0
    for j, size in enumerate(PARTS):
        for n in range(size):
            a_in[t].wait()
            target = outs[j].at[pl.ds((0 if j else head) + n * k, k)]
            copies.append(pltpu.make_async_copy(a_buf.at[t], target, out_sems.at[t]))
            copies[-1].start()
            t += 1
    for copy in copies:
        copy.wait()


def prepare(first, blocks, q, codes):
    _, k, side, _ = blocks.shape
    head, groups = q.size // side**2 + 1, sum(PARTS)
    counts = [size * k + (0 if j else head) for j, size in enumerate(PARTS)]
    found = pl.pallas_call(
        prepare_kernel,
        in_specs=[SMEM, HBM, HBM, VMEM],
        out_specs=[VMEM] + [HBM] * len(PARTS),
        out_shape=[jax.ShapeDtypeStruct((head, side, side), BF16)]
        + [pltpu.HBM((count, side, side), blocks.dtype) for count in counts],
        scratch_shapes=[
            pltpu.VMEM((groups, k, side, side), blocks.dtype),
            pltpu.VMEM(q.shape, q.dtype),
            pltpu.SemaphoreType.DMA((groups + 1,)),
            pltpu.SemaphoreType.DMA((groups + 1,)),
        ],
        compiler_params=params(8),
        name="prepare",
    )(
        first,
        pltpu.with_memory_space_constraint(blocks, pltpu.HBM),
        pltpu.with_memory_space_constraint(q, pltpu.HBM),
        codes,
    )
    return found[0], found[1:]


def slots_kernel(owners, capacity, owner_ref, _, slot_ref):
    owner = owner_ref[...]
    rows = owner.shape[1]
    member = lax.broadcasted_iota(jnp.int32, (owners, rows), 0) == owner
    earlier = lax.broadcasted_iota(jnp.int32, (rows, rows), 0) < lax.broadcasted_iota(jnp.int32, (rows, rows), 1)
    before = jnp.dot(member.astype(BF16), earlier.astype(BF16), preferred_element_type=F32)
    rank = jnp.sum(jnp.where(member, before, 0.0), axis=0, keepdims=True)
    slot_ref[...] = owner * capacity + rank.astype(jnp.int32)


def slots_of(owner, owners, capacity, before):
    return pl.pallas_call(
        functools.partial(slots_kernel, owners, capacity),
        in_specs=[VMEM, ANY],
        out_specs=VMEM,
        out_shape=jax.ShapeDtypeStruct(owner.shape, jnp.int32),
        compiler_params=params(6),
        name="slots",
    )(owner, before)


def fill(d_ref, codes, source, block):
    k, side, at_first = block
    per = d_ref.shape[1] // side
    d_ref[...] = jnp.zeros(d_ref.shape, d_ref.dtype)
    for n in range(k):
        code = codes[source * k + n]
        place = (
            0,
            pl.ds(pl.multiple_of((code // per) * side, side), side),
            pl.ds(pl.multiple_of((code % per) * side, side), side),
        )
        d_ref[place] = (d_ref[place].astype(F32) + at_first(n).astype(F32)).astype(d_ref.dtype)


def turned_dot(q_ref, d_ref, width):
    side = q_ref.shape[1]
    per = d_ref.shape[1] // side
    q = jnp.concatenate(
        [jnp.concatenate([q_ref[i * per + j] for j in range(per)], axis=1) for i in range(width // side)], axis=0
    )
    return jnp.dot(q, d_ref[0], preferred_element_type=F32)


def own_kernel(first_ref, codes_ref, q_ref, a_ref, c_ref, d_ref):
    fill(d_ref, codes_ref, first_ref[0] + pl.program_id(0), (a_ref.shape[1], a_ref.shape[2], lambda n: a_ref[0, n]))
    c_ref[0] = turned_dot(q_ref, d_ref, c_ref.shape[1])


def own_strips(first, codes, q, blocks, shape):
    _, k, side, _ = blocks.shape
    rows, width = shape
    groups = sum(PARTS)
    return pl.pallas_call(
        own_kernel,
        grid_spec=pltpu.PrefetchScalarGridSpec(
            num_scalar_prefetch=2,
            grid=(groups,),
            in_specs=[
                pl.BlockSpec(q.shape, lambda i, *_: (0, 0, 0)),
                pl.BlockSpec((1, k, side, side), lambda i, first, *_: (first[0] + i, 0, 0, 0)),
            ],
            out_specs=[
                pl.BlockSpec((1, width, rows), lambda i, *_: (i, 0, 0)),
                pl.BlockSpec((1, rows, rows), lambda i, *_: (i, 0, 0)),
            ],
        ),
        out_shape=[pltpu.HBM((groups, width, rows), F32), pltpu.HBM((groups, rows, rows), BF16)],
        compiler_params=params(10),
        name="own_strips",
    )(first, codes, q, blocks)


def strip_kernel(start, first_ref, codes_ref, q_ref, b_ref, own_ref, *refs):
    c_ref, d_ref = refs[-2:]
    k = (b_ref.shape[0] - (0 if start else q_ref.shape[0])) // pl.num_programs(0)
    skip = (0 if start else q_ref.shape[0]) + pl.program_id(0) * k
    fill(d_ref, codes_ref, first_ref[0] + start + pl.program_id(0), (k, b_ref.shape[1], lambda n: b_ref[skip + n]))
    c_ref[0] = (own_ref[0] + turned_dot(q_ref, d_ref, c_ref.shape[1])).astype(c_ref.dtype)


def strips(start, size, first, codes, head, opening, received, own, held):
    groups, width, rows = own.shape
    side = opening.shape[1]
    term = pl.BlockSpec((1, width, rows), lambda i, *_: (start + i, 0, 0))
    return pl.pallas_call(
        functools.partial(strip_kernel, start),
        grid_spec=pltpu.PrefetchScalarGridSpec(
            num_scalar_prefetch=2,
            grid=(size,),
            in_specs=[
                pl.BlockSpec((head, side, side), lambda i, *_: (0, 0, 0)),
                pl.BlockSpec(received.shape, lambda i, *_: (0, 0, 0)),
                term,
            ]
            + [HBM] * len(held),
            out_specs=[term, pl.BlockSpec((1, rows, rows), lambda i, *_: (start + i, 0, 0))],
        ),
        out_shape=[pltpu.HBM((groups, width, rows), BF16), pltpu.HBM((groups, rows, rows), BF16)],
        input_output_aliases={5 + n: n for n in range(len(held))},
        compiler_params=params(10),
        name="strips",
    )(first, codes, opening, received, pltpu.with_memory_space_constraint(own, pltpu.HBM), *held)


def forward_kernel(d_ref, p_ref, _, out_ref, total_ref):
    step = pl.program_id(0)
    term = sum(jnp.dot(d_ref[n], p_ref[n], preferred_element_type=F32) for n in range(d_ref.shape[0]))

    @pl.when(step == 0)
    def _():
        total_ref[...] = term

    @pl.when(step > 0)
    def _():
        total_ref[...] += term

    @pl.when(step == pl.num_programs(0) - 1)
    def _():
        out_ref[...] = total_ref[...].astype(out_ref.dtype)


def forward(dense, panels, dtype, before):
    groups, rows, width = panels.shape
    return pl.pallas_call(
        forward_kernel,
        grid=(groups // 2,),
        in_specs=[
            pl.BlockSpec((2, rows, rows), lambda i: (i, 0, 0)),
            pl.BlockSpec((2, rows, width), lambda i: (i, 0, 0)),
            ANY,
        ],
        out_specs=pl.BlockSpec((rows, width), lambda i: (0, 0)),
        scratch_shapes=[pltpu.VMEM((rows, width), F32)],
        out_shape=jax.ShapeDtypeStruct((rows, width), dtype),
        compiler_params=params(12),
        name="forward",
    )(pltpu.with_memory_space_constraint(dense, pltpu.HBM), pltpu.with_memory_space_constraint(panels, pltpu.HBM), before)


def one_hot(slot, slots):
    return (lax.broadcasted_iota(jnp.int32, (slots, slot.shape[1]), 0) == slot).astype(BF16)


def pack_rows_kernel(own_ref, got_ref, slot_ref, samples_ref, packed_ref):
    samples = (own_ref[...] + got_ref[...].astype(F32)).astype(BF16)
    samples_ref[...] = samples
    packed_ref[...] = jnp.dot(
        one_hot(slot_ref[...], packed_ref.shape[0]), samples, preferred_element_type=F32
    ).astype(BF16)


def pack_rows(own, got, slot, slots):
    rows, width = own.shape
    return pl.pallas_call(
        pack_rows_kernel,
        out_shape=[jax.ShapeDtypeStruct((rows, width), BF16), jax.ShapeDtypeStruct((slots, width), BF16)],
        compiler_params=params(8),
        name="pack_rows",
    )(own, got, slot)


def pack_columns_kernel(samples_ref, slot_ref, _, packed_ref, held_ref, sem):
    copy = pltpu.make_async_copy(samples_ref, held_ref, sem)
    copy.start()
    chosen = one_hot(slot_ref[...], packed_ref.shape[0])
    copy.wait()
    packed_ref[...] = lax.dot_general(
        chosen, held_ref[...], (((1,), (1,)), ((), ())), preferred_element_type=F32
    ).astype(BF16)


def pack_columns(samples, slot, slots, before):
    return pl.pallas_call(
        pack_columns_kernel,
        in_specs=[HBM, VMEM, ANY],
        out_specs=VMEM,
        out_shape=jax.ShapeDtypeStruct((slots, samples.shape[0]), BF16),
        scratch_shapes=[pltpu.VMEM(samples.shape, BF16), pltpu.SemaphoreType.DMA],
        compiler_params=params(8),
        name="pack_columns",
    )(pltpu.with_memory_space_constraint(samples, pltpu.HBM), slot, before)


def owner_gram(received, count):
    gram = lax.dot_general(received, received, (((0,), (0,)), ((), ())), preferred_element_type=F32)
    return (gram / count)[None, None]


def body(blocks, block_row, block_col, probes, adjoint_probes, row_owner):
    groups, per_group, side = blocks.shape[2], blocks.shape[3], blocks.shape[4]
    blocks = blocks.reshape(groups, per_group, side, side)
    n_rows, width = probes.shape
    owners = lax.axis_size("grp")
    capacity = 2 * n_rows // owners
    slots = owners * capacity
    ring = groups // 2
    half = lax.axis_index("blk") // ring
    kept, crossing = (half * ring).reshape(1), ((1 - half) * ring).reshape(1)
    across = [(b, (b + ring) % groups) for b in range(groups)]
    halves = [list(range(ring)), list(range(ring, groups))]

    codes = (block_row * (n_rows // side) + block_col).reshape(groups * per_group)
    code_row = jnp.pad(codes.astype(F32), (0, side - codes.shape[0])).reshape(1, side)
    q, leaving = prepare(crossing, blocks, adjoint_probes, code_row)
    panels = lax.all_gather(probes, "blk", axis=0, tiled=True, axis_index_groups=halves).reshape(ring, n_rows, width)
    received = [lax.ppermute(part, "blk", across) for part in leaving]
    partner_codes = received[0][q.shape[0] - 1, 0, 0 : codes.shape[0]].astype(jnp.int32)
    slot = slots_of(row_owner.reshape(1, n_rows), owners, capacity, partner_codes)

    own_terms, own_dense = own_strips(kept, codes, q, blocks, (n_rows, width))
    held = ()
    for j, size in enumerate(PARTS):
        held = strips(
            sum(PARTS[:j]), size, kept, partner_codes, q.shape[0], received[0], received[j], own_terms, held
        )
    terms, dense = held
    columns = lax.psum_scatter(terms, "blk", scatter_dimension=0, tiled=False, axis_index_groups=halves)
    partial = forward(dense, panels, BF16, slot)
    own = forward(own_dense, panels, F32, partial)
    got = lax.ppermute(partial, "blk", across)
    row_samples, row_packed = pack_rows(own, got, slot, slots)
    row_received = lax.all_to_all(row_packed.reshape(owners, capacity, width), "grp", 0, 0, tiled=True)
    column_packed = pack_columns(columns, slot, slots, row_received)
    column_received = lax.all_to_all(column_packed.reshape(owners, capacity, width), "grp", 0, 0, tiled=True)
    row_gram = owner_gram(row_received.reshape(slots, width), n_rows)
    column_gram = owner_gram(column_received.reshape(slots, width), n_rows)
    return (row_samples, columns.T, row_gram, column_gram)


def solution(mesh):
    in_specs = (
        P("blk", "grp", None, None, None, None),
        P("blk", "grp", None, None),
        P("blk", "grp", None, None),
        P(("blk", "grp"), None),
        P(("blk", "grp"), None),
        P(("blk", "grp"), None),
    )
    out_specs = (
        P(("blk", "grp"), None),
        P(("blk", "grp"), None),
        P("blk", "grp", None, None),
        P("blk", "grp", None, None),
    )
    return jax.shard_map(body, mesh=mesh, in_specs=in_specs, out_specs=out_specs, check_vma=False)
```

```python
import functools

import jax
import jax.numpy as jnp
from jax import lax
from jax.experimental import pallas as pl
from jax.experimental.pallas import tpu as pltpu
from jax.sharding import PartitionSpec as P

F32 = jnp.float32
BF16 = jnp.bfloat16
PARTS = (3, 3, 1, 1)


def params(mib):
    return pltpu.CompilerParams(vmem_limit_bytes=mib * 1024 * 1024)


ANY = pl.BlockSpec(memory_space=pl.ANY)
VMEM = pl.BlockSpec(memory_space=pltpu.VMEM)
SMEM = pl.BlockSpec(memory_space=pltpu.SMEM)
HBM = pl.BlockSpec(memory_space=pltpu.HBM)


def prepare_kernel(first_ref, a_ref, q_ref, code_ref, own_ref, *refs):
    outs, (a_buf, q_buf, in_sems, out_sems) = refs[:-4], refs[-4:]
    k, side = a_buf.shape[1:3]
    head, groups = own_ref.shape[0], a_buf.shape[0]
    q_in = pltpu.make_async_copy(q_ref, q_buf, in_sems.at[groups])
    a_in = [pltpu.make_async_copy(a_ref.at[first_ref[0] + t], a_buf.at[t], in_sems.at[t]) for t in range(groups)]
    for copy in [q_in] + a_in:
        copy.start()
    q_in.wait()
    down, across = q_buf.shape[1] // side, q_buf.shape[0] // side
    for i in range(down):
        for j in range(across):
            own_ref[i * across + j] = q_buf[j * side : (j + 1) * side, i * side : (i + 1) * side].T
    own_ref[down * across] = jnp.broadcast_to(code_ref[...], (side, side)).astype(BF16)
    copies = [pltpu.make_async_copy(own_ref, outs[0].at[pl.ds(0, head)], out_sems.at[groups])]
    copies[0].start()
    t = 0
    for j, size in enumerate(PARTS):
        for n in range(size):
            a_in[t].wait()
            target = outs[j].at[pl.ds((0 if j else head) + n * k, k)]
            copies.append(pltpu.make_async_copy(a_buf.at[t], target, out_sems.at[t]))
            copies[-1].start()
            t += 1
    for copy in copies:
        copy.wait()


def prepare(first, blocks, q, codes):
    _, k, side, _ = blocks.shape
    head, groups = q.size // side**2 + 1, sum(PARTS)
    counts = [size * k + (0 if j else head) for j, size in enumerate(PARTS)]
    found = pl.pallas_call(
        prepare_kernel,
        in_specs=[SMEM, HBM, HBM, VMEM],
        out_specs=[VMEM] + [HBM] * len(PARTS),
        out_shape=[jax.ShapeDtypeStruct((head, side, side), BF16)]
        + [pltpu.HBM((count, side, side), blocks.dtype) for count in counts],
        scratch_shapes=[
            pltpu.VMEM((groups, k, side, side), blocks.dtype),
            pltpu.VMEM(q.shape, q.dtype),
            pltpu.SemaphoreType.DMA((groups + 1,)),
            pltpu.SemaphoreType.DMA((groups + 1,)),
        ],
        compiler_params=params(8),
        name="prepare",
    )(
        first,
        pltpu.with_memory_space_constraint(blocks, pltpu.HBM),
        pltpu.with_memory_space_constraint(q, pltpu.HBM),
        codes,
    )
    return found[0], found[1:]


def slots_kernel(owners, capacity, owner_ref, _, slot_ref):
    owner = owner_ref[...]
    rows = owner.shape[1]
    member = lax.broadcasted_iota(jnp.int32, (owners, rows), 0) == owner
    earlier = lax.broadcasted_iota(jnp.int32, (rows, rows), 0) < lax.broadcasted_iota(jnp.int32, (rows, rows), 1)
    before = jnp.dot(member.astype(BF16), earlier.astype(BF16), preferred_element_type=F32)
    rank = jnp.sum(jnp.where(member, before, 0.0), axis=0, keepdims=True)
    slot_ref[...] = owner * capacity + rank.astype(jnp.int32)


def slots_of(owner, owners, capacity, before):
    return pl.pallas_call(
        functools.partial(slots_kernel, owners, capacity),
        in_specs=[VMEM, ANY],
        out_specs=VMEM,
        out_shape=jax.ShapeDtypeStruct(owner.shape, jnp.int32),
        compiler_params=params(6),
        name="slots",
    )(owner, before)


def fill(d_ref, codes, source, block):
    k, side, at_first = block
    per = d_ref.shape[1] // side
    d_ref[...] = jnp.zeros(d_ref.shape, d_ref.dtype)
    for n in range(k):
        code = codes[source * k + n]
        place = (
            0,
            pl.ds(pl.multiple_of((code // per) * side, side), side),
            pl.ds(pl.multiple_of((code % per) * side, side), side),
        )
        d_ref[place] = (d_ref[place].astype(F32) + at_first(n).astype(F32)).astype(d_ref.dtype)


def turned_dot(q_ref, d_ref, width):
    side = q_ref.shape[1]
    per = d_ref.shape[1] // side
    q = jnp.concatenate(
        [jnp.concatenate([q_ref[i * per + j] for j in range(per)], axis=1) for i in range(width // side)], axis=0
    )
    return jnp.dot(q, d_ref[0], preferred_element_type=F32)


def own_kernel(first_ref, codes_ref, q_ref, a_ref, c_ref, d_ref):
    fill(d_ref, codes_ref, first_ref[0] + pl.program_id(0), (a_ref.shape[1], a_ref.shape[2], lambda n: a_ref[0, n]))
    c_ref[0] = turned_dot(q_ref, d_ref, c_ref.shape[1])


def own_strips(first, codes, q, blocks, shape):
    _, k, side, _ = blocks.shape
    rows, width = shape
    groups = sum(PARTS)
    return pl.pallas_call(
        own_kernel,
        grid_spec=pltpu.PrefetchScalarGridSpec(
            num_scalar_prefetch=2,
            grid=(groups,),
            in_specs=[
                pl.BlockSpec(q.shape, lambda i, *_: (0, 0, 0)),
                pl.BlockSpec((1, k, side, side), lambda i, first, *_: (first[0] + i, 0, 0, 0)),
            ],
            out_specs=[
                pl.BlockSpec((1, width, rows), lambda i, *_: (i, 0, 0)),
                pl.BlockSpec((1, rows, rows), lambda i, *_: (i, 0, 0)),
            ],
        ),
        out_shape=[pltpu.HBM((groups, width, rows), F32), pltpu.HBM((groups, rows, rows), BF16)],
        compiler_params=params(10),
        name="own_strips",
    )(first, codes, q, blocks)


def strip_kernel(start, first_ref, codes_ref, q_ref, b_ref, own_ref, *refs):
    c_ref, d_ref = refs[-2:]
    k = (b_ref.shape[0] - (0 if start else q_ref.shape[0])) // pl.num_programs(0)
    skip = (0 if start else q_ref.shape[0]) + pl.program_id(0) * k
    fill(d_ref, codes_ref, first_ref[0] + start + pl.program_id(0), (k, b_ref.shape[1], lambda n: b_ref[skip + n]))
    c_ref[0] = (own_ref[0] + turned_dot(q_ref, d_ref, c_ref.shape[1])).astype(c_ref.dtype)


def strips(start, size, first, codes, head, opening, received, own, held):
    groups, width, rows = own.shape
    side = opening.shape[1]
    term = pl.BlockSpec((1, width, rows), lambda i, *_: (start + i, 0, 0))
    return pl.pallas_call(
        functools.partial(strip_kernel, start),
        grid_spec=pltpu.PrefetchScalarGridSpec(
            num_scalar_prefetch=2,
            grid=(size,),
            in_specs=[
                pl.BlockSpec((head, side, side), lambda i, *_: (0, 0, 0)),
                pl.BlockSpec(received.shape, lambda i, *_: (0, 0, 0)),
                term,
            ]
            + [HBM] * len(held),
            out_specs=[term, pl.BlockSpec((1, rows, rows), lambda i, *_: (start + i, 0, 0))],
        ),
        out_shape=[pltpu.HBM((groups, width, rows), BF16), pltpu.HBM((groups, rows, rows), BF16)],
        input_output_aliases={5 + n: n for n in range(len(held))},
        compiler_params=params(10),
        name="strips",
    )(first, codes, opening, received, pltpu.with_memory_space_constraint(own, pltpu.HBM), *held)


def forward_kernel(d_ref, p_ref, _, out_ref, total_ref):
    step = pl.program_id(0)
    term = sum(jnp.dot(d_ref[n], p_ref[n], preferred_element_type=F32) for n in range(d_ref.shape[0]))

    @pl.when(step == 0)
    def _():
        total_ref[...] = term

    @pl.when(step > 0)
    def _():
        total_ref[...] += term

    @pl.when(step == pl.num_programs(0) - 1)
    def _():
        out_ref[...] = total_ref[...].astype(out_ref.dtype)


def forward(dense, panels, dtype, before):
    groups, rows, width = panels.shape
    return pl.pallas_call(
        forward_kernel,
        grid=(groups // 2,),
        in_specs=[
            pl.BlockSpec((2, rows, rows), lambda i: (i, 0, 0)),
            pl.BlockSpec((2, rows, width), lambda i: (i, 0, 0)),
            ANY,
        ],
        out_specs=pl.BlockSpec((rows, width), lambda i: (0, 0)),
        scratch_shapes=[pltpu.VMEM((rows, width), F32)],
        out_shape=jax.ShapeDtypeStruct((rows, width), dtype),
        compiler_params=params(12),
        name="forward",
    )(pltpu.with_memory_space_constraint(dense, pltpu.HBM), pltpu.with_memory_space_constraint(panels, pltpu.HBM), before)


def one_hot(slot, slots):
    return (lax.broadcasted_iota(jnp.int32, (slots, slot.shape[1]), 0) == slot).astype(BF16)


def pack_rows_kernel(own_ref, got_ref, slot_ref, samples_ref, packed_ref):
    samples = (own_ref[...] + got_ref[...].astype(F32)).astype(BF16)
    samples_ref[...] = samples
    packed_ref[...] = jnp.dot(
        one_hot(slot_ref[...], packed_ref.shape[0]), samples, preferred_element_type=F32
    ).astype(BF16)


def pack_rows(own, got, slot, slots):
    rows, width = own.shape
    return pl.pallas_call(
        pack_rows_kernel,
        out_shape=[jax.ShapeDtypeStruct((rows, width), BF16), jax.ShapeDtypeStruct((slots, width), BF16)],
        compiler_params=params(8),
        name="pack_rows",
    )(own, got, slot)


def pack_columns_kernel(samples_ref, slot_ref, _, packed_ref, held_ref, sem):
    copy = pltpu.make_async_copy(samples_ref, held_ref, sem)
    copy.start()
    chosen = one_hot(slot_ref[...], packed_ref.shape[0])
    copy.wait()
    packed_ref[...] = lax.dot_general(
        chosen, held_ref[...], (((1,), (1,)), ((), ())), preferred_element_type=F32
    ).astype(BF16)


def pack_columns(samples, slot, slots, before):
    return pl.pallas_call(
        pack_columns_kernel,
        in_specs=[HBM, VMEM, ANY],
        out_specs=VMEM,
        out_shape=jax.ShapeDtypeStruct((slots, samples.shape[0]), BF16),
        scratch_shapes=[pltpu.VMEM(samples.shape, BF16), pltpu.SemaphoreType.DMA],
        compiler_params=params(8),
        name="pack_columns",
    )(pltpu.with_memory_space_constraint(samples, pltpu.HBM), slot, before)


def owner_gram(received, count):
    gram = lax.dot_general(received, received, (((0,), (0,)), ((), ())), preferred_element_type=F32)
    return (gram / count)[None, None]


def body(blocks, block_row, block_col, probes, adjoint_probes, row_owner):
    groups, per_group, side = blocks.shape[2], blocks.shape[3], blocks.shape[4]
    blocks = blocks.reshape(groups, per_group, side, side)
    n_rows, width = probes.shape
    owners = lax.axis_size("grp")
    capacity = 2 * n_rows // owners
    slots = owners * capacity
    ring = groups // 2
    half = lax.axis_index("blk") // ring
    kept, crossing = (half * ring).reshape(1), ((1 - half) * ring).reshape(1)
    across = [(b, (b + ring) % groups) for b in range(groups)]
    halves = [list(range(ring)), list(range(ring, groups))]

    codes = (block_row * (n_rows // side) + block_col).reshape(groups * per_group)
    code_row = jnp.pad(codes.astype(F32), (0, side - codes.shape[0])).reshape(1, side)
    q, leaving = prepare(crossing, blocks, adjoint_probes, code_row)
    panels = lax.all_gather(probes, "blk", axis=0, tiled=True, axis_index_groups=halves).reshape(ring, n_rows, width)
    received = [lax.ppermute(part, "blk", across) for part in leaving]
    partner_codes = received[0][q.shape[0] - 1, 0, 0 : codes.shape[0]].astype(jnp.int32)
    slot = slots_of(row_owner.reshape(1, n_rows), owners, capacity, partner_codes)

    own_terms, own_dense = own_strips(kept, codes, q, blocks, (n_rows, width))
    held = ()
    for j, size in enumerate(PARTS):
        held = strips(
            sum(PARTS[:j]), size, kept, partner_codes, q.shape[0], received[0], received[j], own_terms, held
        )
    terms, dense = held
    columns = lax.psum_scatter(terms, "blk", scatter_dimension=0, tiled=False, axis_index_groups=halves)
    partial = forward(dense, panels, BF16, slot)
    own = forward(own_dense, panels, F32, partial)
    got = lax.ppermute(partial, "blk", across)
    row_samples, row_packed = pack_rows(own, got, slot, slots)
    row_received = lax.all_to_all(row_packed.reshape(owners, capacity, width), "grp", 0, 0, tiled=True)
    column_packed = pack_columns(columns, slot, slots, row_received)
    column_received = lax.all_to_all(column_packed.reshape(owners, capacity, width), "grp", 0, 0, tiled=True)
    row_gram = owner_gram(row_received.reshape(slots, width), n_rows)
    column_gram = owner_gram(column_received.reshape(slots, width), n_rows)
    return (row_samples, columns.T, row_gram, column_gram)


def solution(mesh):
    in_specs = (
        P("blk", "grp", None, None, None, None),
        P("blk", "grp", None, None),
        P("blk", "grp", None, None),
        P(("blk", "grp"), None),
        P(("blk", "grp"), None),
        P(("blk", "grp"), None),
    )
    out_specs = (
        P(("blk", "grp"), None),
        P(("blk", "grp"), None),
        P("blk", "grp", None, None),
        P("blk", "grp", None, None),
    )
    return jax.shard_map(body, mesh=mesh, in_specs=in_specs, out_specs=out_specs, check_vma=False)
```
